32 devices in a mesh: parts: 2 (over y), node: 4 (over z), chan: 2 (over x), rep: 2 (over core).
Axes of the slice: x: 2, y: 2, z: 4, core: 2. Of those that a mesh axis runs over, the one named last changes fastest.
Arguments:
- features: float32 [128, 32768], P('chan', ('parts', 'node')), parts along dimension 1, may hold values from -6 to 6
- tile_rows: int32 [2048], P(('parts', 'node', 'rep')), parts along dimension 0, may hold values from 0 to 31
- tile_slot: int32 [2048], P(('parts', 'node', 'rep')), parts along dimension 0, may hold values from 0 to 23, as said below
- slot_block: int32 [16, 24], P(('parts', 'node', 'rep')), parts along dimension 0, may hold values from -1 to 11, as said below
- tiles: int32 [2048, 8, 128], P(('parts', 'node', 'rep')), parts along dimension 0, may hold values from 0 to 65535, as said below
Outputs:
- propagated: float32 [128, 32768], P('chan', ('parts', 'node')), parts along dimension 1
The draws below stay inside these ranges and needn't reach their ends.
There are 2 independent parts, one for each index of `parts`. The reference program is written for one: setup_inputs(seed, part) draws one part's arguments, and reference() takes and returns one part's arrays. A program takes and returns all parts, laid end to end along the dimension named above; each array names one. Nothing has to cross between parts.
Inputs may be any that keep to these rules, and one draw needn't show every extreme that they name: tile_slot // 6 is the owning node index of the tile's hyperedge block; slot_block of the tile's device at that slot is never -1. `slot_block`: for each device and owner, the live slots come first and name different blocks; -1 marks an unused slot; every device's slots for its own node index are all live. `tiles`: word w of column j holds node 16 * w + k in bit k.
All inputs are finite; a program needn't handle non-finite values.
Results may differ from the reference program's by a relative error of at most 0.0001.
Values sent between devices are 32-bit elements; how exact they have to be, the bound alone decides.
A program may use at most 64 MiB of HBM per device.

```python
import math
import jax
import jax.numpy as jnp
import numpy as np
from jax import lax

CH = 128
NODE_DEV = 4096
EB_DEV = 12
CAP = 6
TILES_DEV = 128
ROUNDS = 2
NODES = 16384
TILE_ALL = 1024
N_NODE = 4
N_REP = 2


def slot_layout(key):
    devices = N_NODE * N_REP
    key_count, key_perm, key_owner, key_home, key_slot = jax.random.split(key, 5)
    counts = jax.random.randint(key_count, (devices, N_NODE), 1, CAP + 1)
    home = jnp.arange(devices, dtype=jnp.int32) // N_REP
    counts = jnp.where(jnp.arange(N_NODE, dtype=jnp.int32)[None, :] == home[:, None], CAP, counts)
    perm_keys = jax.random.split(key_perm, devices * N_NODE)
    perms = jax.vmap(lambda k: jax.random.permutation(k, EB_DEV))(perm_keys).astype(jnp.int32)
    perms = perms.reshape(devices, N_NODE, EB_DEV)[:, :, :CAP]
    live = jnp.arange(CAP, dtype=jnp.int32)[None, None, :] < counts[:, :, None]
    blocks = jnp.where(live, perms, -1).reshape(devices, N_NODE * CAP).astype(jnp.int32)
    at_home = jax.random.randint(key_home, (devices, TILES_DEV), 0, 2) == 0
    anywhere = jax.random.randint(key_owner, (devices, TILES_DEV), 0, N_NODE)
    owner = jnp.where(at_home, home[:, None], anywhere)
    limit = jnp.take_along_axis(counts, owner, 1)
    within = jax.random.randint(key_slot, (devices, TILES_DEV), 0, limit)
    slots = (owner * CAP + within).reshape(devices * TILES_DEV).astype(jnp.int32)
    return (blocks, slots)


def draw_tile_slot(key, part):
    return slot_layout(key)[1]


def draw_slot_block(key, part):
    return slot_layout(key)[0]


def draw_tiles(key, part):
    key = jax.random.fold_in(key, 7)
    weights = jnp.left_shift(jnp.ones((16,), jnp.int32), jnp.arange(16, dtype=jnp.int32))

    def one_tile(tile_key):
        ones = (jax.random.randint(tile_key, (128, 128), 0, 96) == 0).astype(jnp.int32)
        grouped = ones.reshape(8, 16, 128)
        return jnp.sum(grouped * weights[None, :, None], axis=1).astype(jnp.int32)
    return lax.map(one_tile, jax.random.split(key, TILE_ALL))


def with_ends(array, stream_key, least, largest):
    shape = array.shape
    spot = [jax.random.randint(jax.random.fold_in(stream_key, axis), (), 0, shape[axis]) for axis in range(len(shape))]
    array = array.at[tuple(spot)].set(least)
    longest = shape.index(max(shape))
    spot[longest] = (spot[longest] + 1) % shape[longest]
    return array.at[tuple(spot)].set(largest)


def shard_levels(key, dims, shards, smallest, top_value):
    loudness = 1.0
    for axis_at, parts in shards:
        draws = jax.random.uniform(jax.random.fold_in(jax.random.fold_in(key, 6), axis_at), (parts,), jnp.float32, smallest / len(shards), top_value / len(shards))
        loudness = loudness * jnp.repeat(jnp.exp(draws), dims[axis_at] // parts).reshape((-1,) + (1,) * (len(dims) - 1 - axis_at))
    return loudness


def normal_values(stream_key, extent, spread, reach, cuts=(), kind=jnp.bfloat16):
    entries = jax.random.normal(stream_key, extent, jnp.float32) * spread
    if len(cuts) > 0:
        entries = shard_levels(stream_key, extent, cuts, -0.22, 0.18) * entries
    return jnp.clip(entries, min=-reach, max=reach).astype(kind)


def setup_inputs(seed: int = 0, part: int = 0) -> dict:
    key_list = jax.random.split(jax.random.key(seed), 6)
    part_splits = jax.random.split(jax.random.fold_in(key_list[5], part), 6)
    features = normal_values(part_splits[0], (CH, NODES), 1.0, 6.0, ((0, 2), (1, 4)), jnp.float32)
    tile_rows = with_ends(jax.random.randint(part_splits[1], (TILE_ALL,), 0, NODE_DEV // 128), jax.random.fold_in(part_splits[1], 1), 0, (NODE_DEV // 128) - 1).astype(jnp.int32)
    tile_slot = draw_tile_slot(jax.random.fold_in(jax.random.fold_in(key_list[5], part), 71), part)
    slot_block = draw_slot_block(jax.random.fold_in(jax.random.fold_in(key_list[5], part), 71), part)
    tiles = draw_tiles(jax.random.fold_in(jax.random.fold_in(key_list[5], part), 71), part)
    return {"features": features, "tile_rows": tile_rows, "tile_slot": tile_slot, "slot_block": slot_block, "tiles": tiles}


highest = lax.Precision.HIGHEST
teleport = 0.1


def unpack(packed):
    word_of = np.arange(128) // 16
    shift_of = jnp.asarray(np.arange(128) % 16, dtype=jnp.int32)
    words = packed[:, word_of, :]
    return jnp.bitwise_and(jnp.right_shift(words, shift_of[None, :, None]), 1).astype(jnp.float32)


def reference(features, tile_rows, tile_slot, slot_block, tiles):
    nblocks = NODE_DEV // 128
    total_blocks = nblocks * N_NODE
    edge_blocks = EB_DEV * N_NODE
    tile_count = tile_rows.shape[0]
    group_size = math.gcd(tile_count, 256)
    turns = tile_count // group_size
    device = jnp.arange(tile_count, dtype=jnp.int32) // TILES_DEV
    node_block = (device // N_REP) * nblocks + tile_rows
    local_block = slot_block[device, tile_slot]
    usable = (local_block >= 0).astype(jnp.float32)
    edge_block = (tile_slot // CAP) * EB_DEV + jnp.maximum(local_block, 0)
    grouped = (tiles.reshape(turns, group_size, 8, 128), node_block.reshape(turns, group_size),
               edge_block.reshape(turns, group_size), usable.reshape(turns, group_size))

    def count_step(carry, inputs):
        packed, node_ids, edge_ids, weight = inputs
        matrices = unpack(packed)
        node_deg = carry[0] + jax.ops.segment_sum(jnp.sum(matrices, 2), node_ids, total_blocks)
        edge_deg = carry[1] + jax.ops.segment_sum(jnp.sum(matrices, 1) * weight[:, None], edge_ids, edge_blocks)
        return (node_deg, edge_deg), None

    start = (jnp.zeros((total_blocks, 128), jnp.float32), jnp.zeros((edge_blocks, 128), jnp.float32))
    node_degree, edge_degree = lax.scan(count_step, start, grouped)[0]
    anchor = features.reshape(CH, total_blocks, 128).transpose(1, 0, 2)
    current = anchor
    for turn_index in range(ROUNDS):
        def push_step(running, inputs, source=current):
            packed, node_ids, edge_ids, weight = inputs
            matrices = unpack(packed)
            picked = source[node_ids]
            product = jnp.einsum('tcn,tne->tce', picked, matrices, precision=highest) * weight[:, None, None]
            return running + jax.ops.segment_sum(product, edge_ids, edge_blocks), None

        edge_sum = lax.scan(push_step, jnp.zeros((edge_blocks, CH, 128), jnp.float32), grouped)[0]
        edge_mean = edge_sum / jnp.maximum(edge_degree, 1.0)[:, None, :]

        def pull_step(running, inputs, means=edge_mean):
            packed, node_ids, edge_ids, weight = inputs
            matrices = unpack(packed)
            values = means[edge_ids] * weight[:, None, None]
            contrib = jnp.einsum('tce,tne->tcn', values, matrices, precision=highest)
            return running + jax.ops.segment_sum(contrib, node_ids, total_blocks), None

        node_sum = lax.scan(pull_step, jnp.zeros((total_blocks, CH, 128), jnp.float32), grouped)[0]
        node_mean = node_sum / jnp.maximum(node_degree, 1.0)[:, None, :]
        current = (1.0 - teleport) * node_mean + teleport * anchor
    return current.transpose(1, 0, 2).reshape(CH, NODES)
```

```python
import functools

import jax
import jax.numpy as jnp
from jax import lax
from jax.experimental import pallas as pl
from jax.experimental.pallas import tpu as pltpu
from jax.sharding import PartitionSpec as P

EB_DEV = 12
CAP = 6
ROUNDS = 2
CHUNKS = 8
OUT_CHUNKS = 4
UNROLL = 8
MESH = pl.DeviceIdType.MESH
teleport = 0.1


def split_rows(value, ones):
    high = value.astype(jnp.bfloat16).astype(jnp.float32)
    parts = [high, value - high]
    if ones:
        parts.append(jnp.ones((16, 128), jnp.float32))
    return jnp.concatenate(parts, axis=0).astype(jnp.bfloat16)


def kernel(
    n_node,
    order_e, row_e, keep_e, last_e, order_r, edge_r, keep_r, last_r,
    feat_ref, tiles_ref,
    out_ref,
    tiles_in, unp, xs, ms, run_sums, own, in_left, in_right, to_left, to_right,
    own_deg, deg_left, deg_right, deg_to_left, deg_to_right, node_floor, edge_inv,
    tile_sem, out_send, out_recv, send_l, send_r, recv_l, recv_r, deg_sem,
):
    ch = feat_ref.shape[1]
    tile_count = tiles_ref.shape[0]
    total_tiles = 2 * tile_count
    nblocks = feat_ref.shape[2] // 128
    edge_blocks = own.shape[0]
    per = edge_blocks // CHUNKS
    pos = lax.axis_index("node")
    rep = lax.axis_index("rep")
    left, right = pos - 1, pos + 1
    has_left = pos > 0
    has_right = pos < n_node - 1

    barrier = pltpu.get_barrier_semaphore()
    pl.semaphore_signal(barrier, inc=1, device_id={"rep": 1 - rep}, device_id_type=MESH)

    @pl.when(has_left)
    def _():
        pl.semaphore_signal(barrier, inc=1, device_id={"node": left}, device_id_type=MESH)

    @pl.when(has_right)
    def _():
        pl.semaphore_signal(barrier, inc=1, device_id={"node": right}, device_id_type=MESH)

    pl.semaphore_wait(barrier, 1 + jnp.where(has_left, 1, 0) + jnp.where(has_right, 1, 0))

    tile_copy = pltpu.make_async_remote_copy(
        src_ref=tiles_ref, dst_ref=tiles_in, send_sem=tile_sem.at[0], recv_sem=tile_sem.at[1],
        device_id={"rep": 1 - rep}, device_id_type=MESH,
    )
    tile_copy.start()

    zero_rows = jnp.zeros(run_sums.shape[1:], jnp.float32)
    run_sums[total_tiles] = zero_rows
    bit = jnp.left_shift(1, lax.broadcasted_iota(jnp.int32, (128, 128), 0) & 15)

    def unpack_from(source, base):
        def body(t, _):
            packed = source[t]
            words = jnp.broadcast_to(packed[:, None, :], (8, 16, 128)).reshape(128, 128)
            ones = jnp.where((words & bit) != 0, 1.0, 0.0)
            unp[base + t] = ones.astype(jnp.bfloat16)
            return 0

        lax.fori_loop(0, tile_count, body, 0, unroll=4)

    def load_features(r, _):
        block = feat_ref[rep, :, pl.ds(pl.multiple_of(r * 128, 128), 128)]
        xs[r] = split_rows(block, True)
        return 0

    lax.fori_loop(0, nblocks, load_features, 0, unroll=2)
    unpack_from(tiles_ref, 0)
    tile_copy.wait()
    unpack_from(tiles_in, tile_count)

    def sweep(order, source_of, keep, source, transposed, first):
        rows = 2 * ch + (16 if first else 0)
        dims = (((1,), (1 if transposed else 0,)), ((), ()))

        def step(t, running):
            product = lax.dot_general(
                source[source_of[t]][:rows], unp[order[t]], dims,
                preferred_element_type=jnp.float32,
            )
            fresh = product[:ch] + product[ch:2 * ch]
            if first:
                fresh = jnp.concatenate([fresh, product[2 * ch:2 * ch + 8]], axis=0)
            running = running * keep[t] + fresh
            run_sums[t, :ch + (8 if first else 0)] = running
            return running

        start = jnp.zeros((ch + (8 if first else 0), 128), jnp.float32)
        lax.fori_loop(0, total_tiles, step, start, unroll=UNROLL)

    def remote(source, target, send, recv, where):
        return pltpu.make_async_remote_copy(
            src_ref=source, dst_ref=target, send_sem=send, recv_sem=recv,
            device_id={"node": where}, device_id_type=MESH,
        )

    def chunk_copies(turn, k):
        part = pl.ds(k * per, per)
        go_right = remote(to_right.at[turn, part], in_left.at[turn, part],
                          send_r.at[turn, k], recv_l.at[turn, k], right)
        go_left = remote(to_left.at[turn, part], in_right.at[turn, part],
                         send_l.at[turn, k], recv_r.at[turn, k], left)
        return part, go_right, go_left

    def zero_ends(turn):
        @pl.when(jnp.logical_not(has_left))
        def _():
            in_left[turn] = jnp.zeros(in_left.shape[1:], jnp.float32)
            deg_left[...] = jnp.zeros_like(deg_left)

        @pl.when(jnp.logical_not(has_right))
        def _():
            in_right[turn] = jnp.zeros(in_right.shape[1:], jnp.float32)
            deg_right[...] = jnp.zeros_like(deg_right)

    def forward(turn, k):
        part, go_right, go_left = chunk_copies(turn, k)

        @pl.when(has_left)
        def _():
            go_right.wait_recv()

        @pl.when(has_right)
        def _():
            to_right[turn, part] = own[part] + in_left[turn, part]
            go_right.start()
            go_left.wait_recv()

        @pl.when(has_left)
        def _():
            to_left[turn, part] = own[part] + in_right[turn, part]
            go_left.start()

    def forward_degrees():
        go_right = remote(deg_to_right, deg_left, deg_sem.at[0], deg_sem.at[1], right)
        go_left = remote(deg_to_left, deg_right, deg_sem.at[2], deg_sem.at[3], left)

        @pl.when(has_left)
        def _():
            go_right.wait_recv()

        @pl.when(has_right)
        def _():
            deg_to_right[...] = own_deg[...] + deg_left[...]
            go_right.start()
            go_left.wait_recv()

        @pl.when(has_left)
        def _():
            deg_to_left[...] = own_deg[...] + deg_right[...]
            go_left.start()

        degree = own_deg[...] + deg_left[...] + deg_right[...]
        edge_inv[...] = 1.0 / jnp.maximum(degree, 1.0)

        @pl.when(has_right)
        def _():
            go_right.wait_send()

        @pl.when(has_left)
        def _():
            go_left.wait_send()

    for turn in range(ROUNDS):
        first = turn == 0
        zero_ends(turn)
        sweep(order_e, row_e, keep_e, xs, False, first)

        def take_edges(b, _, first=first):
            found = run_sums[last_e[b]]
            own[b] = found[:ch]
            if first:
                own_deg[b] = found[ch:ch + 8]
            return 0

        lax.fori_loop(0, edge_blocks, take_edges, 0, unroll=4)
        if first:
            forward_degrees()
        for k in range(CHUNKS):
            forward(turn, k)

        def means(b, _, turn=turn, first=first):
            edge_sum = own[b] + in_left[turn, b] + in_right[turn, b]
            ms[b] = split_rows(edge_sum * edge_inv[b, :1], True)
            return 0

        lax.fori_loop(0, edge_blocks, means, 0, unroll=2)
        ms[edge_blocks] = jnp.concatenate(
            [jnp.zeros((2 * ch, 128), jnp.float32), jnp.ones((16, 128), jnp.float32)], axis=0
        ).astype(jnp.bfloat16)

        for k in range(CHUNKS):
            part, go_right, go_left = chunk_copies(turn, k)

            @pl.when(has_right)
            def _():
                go_right.wait_send()

            @pl.when(has_left)
            def _():
                go_left.wait_send()

        sweep(order_r, edge_r, keep_r, ms, True, first)

        def new_block(r, first=first):
            found = run_sums[last_r[r]]
            if first:
                node_floor[r] = jnp.maximum(found[ch:ch + 8], 1.0)
            lanes = pl.ds(pl.multiple_of(r * 128, 128), 128)
            block = feat_ref[rep, :, lanes]
            return lanes, (1.0 - teleport) * (found[:ch] / node_floor[r][:1]) + teleport * block

        if turn < ROUNDS - 1:
            def next_x(r, _):
                xs[r] = split_rows(new_block(r)[1], True)
                return 0

            lax.fori_loop(0, nblocks, next_x, 0, unroll=2)
        else:
            group = nblocks // OUT_CHUNKS
            copies = []
            for k in range(OUT_CHUNKS):
                def last_x(r, _):
                    lanes, value = new_block(r)
                    out_ref[rep, :, lanes] = value
                    return 0

                lax.fori_loop(k * group, (k + 1) * group, last_x, 0, unroll=2)
                span = pl.ds(k * group * 128, group * 128)
                copy = pltpu.make_async_remote_copy(
                    src_ref=out_ref.at[rep, :, span], dst_ref=out_ref.at[rep, :, span],
                    send_sem=out_send.at[k], recv_sem=out_recv.at[k],
                    device_id={"rep": 1 - rep}, device_id_type=MESH,
                )
                copy.start()
                copies.append(copy)
            for copy in copies:
                copy.wait()


def shards(features, tile_rows, tile_slot, slot_block, tiles):
    n_node = lax.axis_size("node")
    channels, row_count = features.shape
    nblocks = row_count // 128
    tile_count = tile_rows.shape[0]
    total = 2 * tile_count
    ch = channels // 2
    edge_blocks = n_node * EB_DEV

    slots = slot_block.reshape(-1)
    slot_of = jnp.arange(slots.shape[0], dtype=jnp.int32)
    slot_edge = jnp.where(slots >= 0, slot_of // CAP * EB_DEV + slots, edge_blocks)
    edges = jnp.sum(jnp.where(tile_slot[:, None] == slot_of[None, :], slot_edge[None, :], 0), axis=1)
    mine = jnp.concatenate([tile_rows, edges.astype(jnp.int32)])
    theirs = lax.ppermute(mine, "rep", [(0, 1), (1, 0)])
    rows = jnp.concatenate([mine[:tile_count], theirs[:tile_count]])
    edges = jnp.concatenate([mine[tile_count:], theirs[tile_count:]])
    ids = jnp.arange(total, dtype=jnp.int32)

    def arrange(key, other, groups):
        full = key * total + ids
        rank = jnp.sum((full[None, :] < full[:, None]).astype(jnp.int32), axis=1)
        hot = rank[None, :] == ids[:, None]
        order = jnp.sum(jnp.where(hot, ids[None, :], 0), axis=1)
        source = jnp.sum(jnp.where(hot, other[None, :], 0), axis=1)
        first = jnp.sum((key[None, :] == key[:, None]) & (full[None, :] < full[:, None]), axis=1) == 0
        keep = jnp.sum(jnp.where(hot & ~first[None, :], 1.0, 0.0), axis=1)
        group = jnp.arange(groups, dtype=jnp.int32)
        upto = jnp.sum((key[None, :] <= group[:, None]).astype(jnp.int32), axis=1)
        some = jnp.any(key[None, :] == group[:, None], axis=1)
        return order, source, keep, jnp.where(some, upto - 1, total)

    order_e, row_e, keep_e, last_e = arrange(edges, rows, edge_blocks)
    order_r, edge_r, keep_r, last_r = arrange(rows, edges, nblocks)

    smem = pl.BlockSpec(memory_space=pltpu.SMEM)
    vmem = pl.BlockSpec(memory_space=pltpu.VMEM)
    f32, bf16 = jnp.float32, jnp.bfloat16
    wide = (edge_blocks, ch, 128)
    deg = (edge_blocks, 8, 128)
    dma = pltpu.SemaphoreType.DMA
    out = pl.pallas_call(
        functools.partial(kernel, n_node),
        out_shape=jax.ShapeDtypeStruct((2, ch, row_count), f32),
        in_specs=[smem] * 8 + [vmem] * 2,
        out_specs=vmem,
        scratch_shapes=[
            pltpu.VMEM((tile_count, 8, 128), jnp.int32),
            pltpu.VMEM((total, 128, 128), bf16),
            pltpu.VMEM((nblocks, 2 * ch + 16, 128), bf16),
            pltpu.VMEM((edge_blocks + 1, 2 * ch + 16, 128), bf16),
            pltpu.VMEM((total + 1, ch + 8, 128), f32),
            pltpu.VMEM(wide, f32),
            pltpu.VMEM((ROUNDS,) + wide, f32),
            pltpu.VMEM((ROUNDS,) + wide, f32),
            pltpu.VMEM((ROUNDS,) + wide, f32),
            pltpu.VMEM((ROUNDS,) + wide, f32),
            pltpu.VMEM(deg, f32),
            pltpu.VMEM(deg, f32),
            pltpu.VMEM(deg, f32),
            pltpu.VMEM(deg, f32),
            pltpu.VMEM(deg, f32),
            pltpu.VMEM((nblocks, 8, 128), f32),
            pltpu.VMEM(deg, f32),
            dma((2,)),
            dma((OUT_CHUNKS,)),
            dma((OUT_CHUNKS,)),
            dma((ROUNDS, CHUNKS)),
            dma((ROUNDS, CHUNKS)),
            dma((ROUNDS, CHUNKS)),
            dma((ROUNDS, CHUNKS)),
            dma((4,)),
        ],
        compiler_params=pltpu.CompilerParams(
            collective_id=0, has_side_effects=True, vmem_limit_bytes=48 * 1024 * 1024
        ),
    )(order_e, row_e, keep_e, last_e, order_r, edge_r, keep_r, last_r,
      features.reshape(2, ch, row_count), tiles)
    return out.reshape(channels, row_count)


def solution(mesh):
    return jax.shard_map(
        shards,
        mesh=mesh,
        in_specs=(
            P("chan", ("parts", "node")),
            P(("parts", "node", "rep")),
            P(("parts", "node", "rep")),
            P(("parts", "node", "rep"), None),
            P(("parts", "node", "rep"), None, None),
        ),
        out_specs=P("chan", ("parts", "node")),
        check_vma=False,
    )
```

```python
import functools

import jax
import jax.numpy as jnp
from jax import lax
from jax.experimental import pallas as pl
from jax.experimental.pallas import tpu as pltpu
from jax.sharding import PartitionSpec as P

EB_DEV = 12
CAP = 6
ROUNDS = 2
CHUNKS = 12
HOP = 2
OUT_CHUNKS = 4
UNROLL = 8
MESH = pl.DeviceIdType.MESH
teleport = 0.1


def split_rows(value, ones):
    high = value.astype(jnp.bfloat16).astype(jnp.float32)
    parts = [high, value - high]
    if ones:
        parts.append(jnp.ones((16, 128), jnp.float32))
    return jnp.concatenate(parts, axis=0).astype(jnp.bfloat16)


def kernel(
    n_node,
    order_e, row_e, keep_e, last_e, order_r, edge_r, keep_r, last_r,
    feat_ref, tiles_ref,
    out_ref,
    tiles_in, unp, xs, ms, run_sums, own, in_left, in_right, to_left, to_right,
    own_deg, deg_left, deg_right, deg_to_left, deg_to_right, node_floor, edge_inv,
    tile_sem, out_send, out_recv, send_l, send_r, recv_l, recv_r, deg_sem,
):
    ch = feat_ref.shape[1]
    tile_count = tiles_ref.shape[0]
    total_tiles = 2 * tile_count
    nblocks = feat_ref.shape[2] // 128
    edge_blocks = own.shape[0]
    per = edge_blocks // CHUNKS
    pos = lax.axis_index("node")
    rep = lax.axis_index("rep")
    left, right = pos - 1, pos + 1
    has_left = pos > 0
    has_right = pos < n_node - 1

    barrier = pltpu.get_barrier_semaphore()
    pl.semaphore_signal(barrier, inc=1, device_id={"rep": 1 - rep}, device_id_type=MESH)

    @pl.when(has_left)
    def _():
        pl.semaphore_signal(barrier, inc=1, device_id={"node": left}, device_id_type=MESH)

    @pl.when(has_right)
    def _():
        pl.semaphore_signal(barrier, inc=1, device_id={"node": right}, device_id_type=MESH)

    pl.semaphore_wait(barrier, 1 + jnp.where(has_left, 1, 0) + jnp.where(has_right, 1, 0))

    tile_copy = pltpu.make_async_remote_copy(
        src_ref=tiles_ref, dst_ref=tiles_in, send_sem=tile_sem.at[0], recv_sem=tile_sem.at[1],
        device_id={"rep": 1 - rep}, device_id_type=MESH,
    )
    tile_copy.start()

    zero_rows = jnp.zeros(run_sums.shape[1:], jnp.float32)
    run_sums[total_tiles] = zero_rows
    bit = jnp.left_shift(1, lax.broadcasted_iota(jnp.int32, (128, 128), 0) & 15)

    def unpack_from(source, base):
        def body(t, _):
            packed = source[t]
            words = jnp.broadcast_to(packed[:, None, :], (8, 16, 128)).reshape(128, 128)
            ones = jnp.where((words & bit) != 0, 1.0, 0.0)
            unp[base + t] = ones.astype(jnp.bfloat16)
            return 0

        lax.fori_loop(0, tile_count, body, 0, unroll=4)

    def load_features(r, _):
        block = feat_ref[rep, :, pl.ds(pl.multiple_of(r * 128, 128), 128)]
        xs[r] = split_rows(block, True)
        return 0

    lax.fori_loop(0, nblocks, load_features, 0, unroll=2)
    unpack_from(tiles_ref, 0)
    tile_copy.wait()
    unpack_from(tiles_in, tile_count)

    def sweep(order, source_of, keep, source, transposed, first):
        rows = 2 * ch + (16 if first else 0)
        dims = (((1,), (1 if transposed else 0,)), ((), ()))

        def step(g, running):
            base = g * UNROLL
            fresh = []
            for u in range(UNROLL):
                product = lax.dot_general(
                    source[source_of[base + u]][:rows], unp[order[base + u]], dims,
                    preferred_element_type=jnp.float32,
                )
                value = product[:ch] + product[ch:2 * ch]
                if first:
                    value = jnp.concatenate([value, product[2 * ch:2 * ch + 8]], axis=0)
                fresh.append(value)
            for u in range(UNROLL):
                running = running * keep[base + u] + fresh[u]
                fresh[u] = running
            for u in range(UNROLL):
                run_sums[base + u, :ch + (8 if first else 0)] = fresh[u]
            return running

        start = jnp.zeros((ch + (8 if first else 0), 128), jnp.float32)
        lax.fori_loop(0, total_tiles // UNROLL, step, start)

    def remote(source, target, send, recv, where):
        return pltpu.make_async_remote_copy(
            src_ref=source, dst_ref=target, send_sem=send, recv_sem=recv,
            device_id={"node": where}, device_id_type=MESH,
        )

    def copy_right(turn, k):
        part = pl.ds(k * per, per)
        return remote(to_right.at[turn, part], in_left.at[turn, part],
                      send_r.at[turn, k], recv_l.at[turn, k], right)

    def copy_left(turn, k):
        part = pl.ds(k * per, per)
        return remote(to_left.at[turn, part], in_right.at[turn, part],
                      send_l.at[turn, k], recv_r.at[turn, k], left)

    deg_right_copy = remote(deg_to_right, deg_left, deg_sem.at[0], deg_sem.at[1], right)
    deg_left_copy = remote(deg_to_left, deg_right, deg_sem.at[2], deg_sem.at[3], left)

    def zero_ends(turn):
        @pl.when(jnp.logical_not(has_left))
        def _():
            in_left[turn] = jnp.zeros(in_left.shape[1:], jnp.float32)
            deg_left[...] = jnp.zeros_like(deg_left)

        @pl.when(jnp.logical_not(has_right))
        def _():
            in_right[turn] = jnp.zeros(in_right.shape[1:], jnp.float32)
            deg_right[...] = jnp.zeros_like(deg_right)

    def pass_on(turn, k, first, sends, receives, copy_of, to_there, from_there, deg_copy,
                deg_to_there, deg_from_there):
        part = pl.ds(k * per, per)

        def degrees_too(act):
            if first:
                pl.when(k == 0)(act)

        @pl.when(receives)
        def _():
            degrees_too(lambda: deg_copy.wait_recv())
            copy_of(turn, k).wait_recv()

        @pl.when(sends)
        def _():
            def send_degrees():
                deg_to_there[...] = own_deg[...] + deg_from_there[...]
                deg_copy.start()

            degrees_too(send_degrees)
            to_there[turn, part] = own[part] + from_there[turn, part]
            copy_of(turn, k).start()

    def exchange(turn, first):
        def step(s, _):
            k_right = s - HOP * pos
            k_left = s - HOP * (n_node - 1 - pos)

            @pl.when((k_right >= 0) & (k_right < CHUNKS))
            def _():
                pass_on(turn, k_right, first, has_right, has_left, copy_right, to_right, in_left,
                        deg_right_copy, deg_to_right, deg_left)

            @pl.when((k_left >= 0) & (k_left < CHUNKS))
            def _():
                pass_on(turn, k_left, first, has_left, has_right, copy_left, to_left, in_right,
                        deg_left_copy, deg_to_left, deg_right)

            return 0

        lax.fori_loop(0, CHUNKS + HOP * (n_node - 1), step, 0)

    for turn in range(ROUNDS):
        first = turn == 0
        zero_ends(turn)
        sweep(order_e, row_e, keep_e, xs, False, first)

        def take_edges(b, _, first=first):
            found = run_sums[last_e[b]]
            own[b] = found[:ch]
            if first:
                own_deg[pl.ds(b, 1)] = found[ch:ch + 1]
            return 0

        lax.fori_loop(0, edge_blocks, take_edges, 0, unroll=4)
        exchange(turn, first)
        if first:
            degree = own_deg[...] + deg_left[...] + deg_right[...]
            edge_inv[...] = 1.0 / jnp.maximum(degree, 1.0)

        def means(b, _, turn=turn, first=first):
            edge_sum = own[b] + in_left[turn, b] + in_right[turn, b]
            ms[b] = split_rows(edge_sum * edge_inv[pl.ds(b, 1)], True)
            return 0

        lax.fori_loop(0, edge_blocks, means, 0, unroll=2)
        ms[edge_blocks] = jnp.concatenate(
            [jnp.zeros((2 * ch, 128), jnp.float32), jnp.ones((16, 128), jnp.float32)], axis=0
        ).astype(jnp.bfloat16)

        def sent(k, _, turn=turn):
            @pl.when(has_right)
            def _():
                copy_right(turn, k).wait_send()

            @pl.when(has_left)
            def _():
                copy_left(turn, k).wait_send()

            return 0

        lax.fori_loop(0, CHUNKS, sent, 0)
        if first:
            @pl.when(has_right)
            def _():
                deg_right_copy.wait_send()

            @pl.when(has_left)
            def _():
                deg_left_copy.wait_send()

        sweep(order_r, edge_r, keep_r, ms, True, first)

        def new_block(r, first=first):
            found = run_sums[last_r[r]]
            if first:
                node_floor[r] = jnp.maximum(found[ch:ch + 8], 1.0)
            lanes = pl.ds(pl.multiple_of(r * 128, 128), 128)
            block = feat_ref[rep, :, lanes]
            return lanes, (1.0 - teleport) * (found[:ch] / node_floor[r][:1]) + teleport * block

        if turn < ROUNDS - 1:
            def next_x(r, _):
                xs[r] = split_rows(new_block(r)[1], True)
                return 0

            lax.fori_loop(0, nblocks, next_x, 0, unroll=2)
        else:
            group = nblocks // OUT_CHUNKS
            copies = []
            for k in range(OUT_CHUNKS):
                def last_x(r, _):
                    lanes, value = new_block(r)
                    out_ref[rep, :, lanes] = value
                    return 0

                lax.fori_loop(k * group, (k + 1) * group, last_x, 0, unroll=2)
                span = pl.ds(k * group * 128, group * 128)
                copy = pltpu.make_async_remote_copy(
                    src_ref=out_ref.at[rep, :, span], dst_ref=out_ref.at[rep, :, span],
                    send_sem=out_send.at[k], recv_sem=out_recv.at[k],
                    device_id={"rep": 1 - rep}, device_id_type=MESH,
                )
                copy.start()
                copies.append(copy)
            for copy in copies:
                copy.wait()


def shards(features, tile_rows, tile_slot, slot_block, tiles):
    n_node = lax.axis_size("node")
    channels, row_count = features.shape
    nblocks = row_count // 128
    tile_count = tile_rows.shape[0]
    total = 2 * tile_count
    ch = channels // 2
    edge_blocks = n_node * EB_DEV

    slots = slot_block.reshape(-1)
    slot_of = jnp.arange(slots.shape[0], dtype=jnp.int32)
    slot_edge = jnp.where(slots >= 0, slot_of // CAP * EB_DEV + slots, edge_blocks)
    edges = jnp.sum(jnp.where(tile_slot[:, None] == slot_of[None, :], slot_edge[None, :], 0), axis=1)
    mine = jnp.concatenate([tile_rows, edges.astype(jnp.int32)])
    theirs = lax.ppermute(mine, "rep", [(0, 1), (1, 0)])
    rows = jnp.concatenate([mine[:tile_count], theirs[:tile_count]])
    edges = jnp.concatenate([mine[tile_count:], theirs[tile_count:]])
    ids = jnp.arange(total, dtype=jnp.int32)

    def arrange(key, other, groups):
        full = key * total + ids
        rank = jnp.sum((full[None, :] < full[:, None]).astype(jnp.int32), axis=1)
        hot = rank[None, :] == ids[:, None]
        order = jnp.sum(jnp.where(hot, ids[None, :], 0), axis=1)
        source = jnp.sum(jnp.where(hot, other[None, :], 0), axis=1)
        first = jnp.sum((key[None, :] == key[:, None]) & (full[None, :] < full[:, None]), axis=1) == 0
        keep = jnp.sum(jnp.where(hot & ~first[None, :], 1.0, 0.0), axis=1)
        group = jnp.arange(groups, dtype=jnp.int32)
        upto = jnp.sum((key[None, :] <= group[:, None]).astype(jnp.int32), axis=1)
        some = jnp.any(key[None, :] == group[:, None], axis=1)
        return order, source, keep, jnp.where(some, upto - 1, total)

    order_e, row_e, keep_e, last_e = arrange(edges, rows, edge_blocks)
    order_r, edge_r, keep_r, last_r = arrange(rows, edges, nblocks)

    smem = pl.BlockSpec(memory_space=pltpu.SMEM)
    vmem = pl.BlockSpec(memory_space=pltpu.VMEM)
    f32, bf16 = jnp.float32, jnp.bfloat16
    wide = (edge_blocks, ch, 128)
    deg = (edge_blocks, 128)
    dma = pltpu.SemaphoreType.DMA
    out = pl.pallas_call(
        functools.partial(kernel, n_node),
        out_shape=jax.ShapeDtypeStruct((2, ch, row_count), f32),
        in_specs=[smem] * 8 + [vmem] * 2,
        out_specs=vmem,
        scratch_shapes=[
            pltpu.VMEM((tile_count, 8, 128), jnp.int32),
            pltpu.VMEM((total, 128, 128), bf16),
            pltpu.VMEM((nblocks, 2 * ch + 16, 128), bf16),
            pltpu.VMEM((edge_blocks + 1, 2 * ch + 16, 128), bf16),
            pltpu.VMEM((total + 1, ch + 8, 128), f32),
            pltpu.VMEM(wide, f32),
            pltpu.VMEM((ROUNDS,) + wide, f32),
            pltpu.VMEM((ROUNDS,) + wide, f32),
            pltpu.VMEM((ROUNDS,) + wide, f32),
            pltpu.VMEM((ROUNDS,) + wide, f32),
            pltpu.VMEM(deg, f32),
            pltpu.VMEM(deg, f32),
            pltpu.VMEM(deg, f32),
            pltpu.VMEM(deg, f32),
            pltpu.VMEM(deg, f32),
            pltpu.VMEM((nblocks, 8, 128), f32),
            pltpu.VMEM(deg, f32),
            dma((2,)),
            dma((OUT_CHUNKS,)),
            dma((OUT_CHUNKS,)),
            dma((ROUNDS, CHUNKS)),
            dma((ROUNDS, CHUNKS)),
            dma((ROUNDS, CHUNKS)),
            dma((ROUNDS, CHUNKS)),
            dma((4,)),
        ],
        compiler_params=pltpu.CompilerParams(
            collective_id=0, has_side_effects=True, vmem_limit_bytes=48 * 1024 * 1024
        ),
    )(order_e, row_e, keep_e, last_e, order_r, edge_r, keep_r, last_r,
      features.reshape(2, ch, row_count), tiles)
    return out.reshape(channels, row_count)


def solution(mesh):
    return jax.shard_map(
        shards,
        mesh=mesh,
        in_specs=(
            P("chan", ("parts", "node")),
            P(("parts", "node", "rep")),
            P(("parts", "node", "rep")),
            P(("parts", "node", "rep"), None),
            P(("parts", "node", "rep"), None, None),
        ),
        out_specs=P("chan", ("parts", "node")),
        check_vma=False,
    )
```

```python
import functools

import jax
import jax.numpy as jnp
from jax import lax
from jax.experimental import pallas as pl
from jax.experimental.pallas import tpu as pltpu
from jax.sharding import PartitionSpec as P

EB_DEV = 12
CAP = 6
ROUNDS = 2
CHUNKS = 16
HOP = 8
OUT_CHUNKS = 2
UNROLL = 32
MESH = pl.DeviceIdType.MESH
teleport = 0.1


def split_rows(value, ones):
    high = value.astype(jnp.bfloat16).astype(jnp.float32)
    parts = [high, value - high]
    if ones:
        parts.append(jnp.ones((16, 128), jnp.float32))
    return jnp.concatenate(parts, axis=0).astype(jnp.bfloat16)


def kernel(
    n_node,
    order_e, row_e, keep_e, last_e, order_r, edge_r, keep_r, last_r,
    feat_ref, tiles_ref,
    out_ref,
    tiles_in, unp, xs, ms, run_sums, own, in_left, in_right, to_left, to_right,
    own_deg, deg_left, deg_right, deg_to_left, deg_to_right, node_floor, edge_inv,
    tile_sem, out_send, out_recv, send_l, send_r, recv_l, recv_r, deg_sem,
):
    halves, ch = feat_ref.shape[1:3]
    tile_count = tiles_ref.shape[0]
    total_tiles = 2 * tile_count
    nblocks = feat_ref.shape[3] // 128
    edge_blocks = own.shape[1]
    per = edge_blocks // CHUNKS
    pos = lax.axis_index("node")
    rep = lax.axis_index("rep")
    left, right = pos - 1, pos + 1
    has_left = pos > 0
    has_right = pos < n_node - 1

    barrier = pltpu.get_barrier_semaphore()
    pl.semaphore_signal(barrier, inc=1, device_id={"rep": 1 - rep}, device_id_type=MESH)

    @pl.when(has_left)
    def _():
        pl.semaphore_signal(barrier, inc=1, device_id={"node": left}, device_id_type=MESH)

    @pl.when(has_right)
    def _():
        pl.semaphore_signal(barrier, inc=1, device_id={"node": right}, device_id_type=MESH)

    pl.semaphore_wait(barrier, 1 + jnp.where(has_left, 1, 0) + jnp.where(has_right, 1, 0))

    tile_copy = pltpu.make_async_remote_copy(
        src_ref=tiles_ref, dst_ref=tiles_in, send_sem=tile_sem.at[0], recv_sem=tile_sem.at[1],
        device_id={"rep": 1 - rep}, device_id_type=MESH,
    )
    tile_copy.start()

    zero_rows = jnp.zeros(run_sums.shape[1:], jnp.float32)
    run_sums[total_tiles] = zero_rows
    bit = jnp.left_shift(1, lax.broadcasted_iota(jnp.int32, (128, 128), 0) & 15)

    def unpack_from(source, base):
        def body(t, _):
            packed = source[t]
            words = jnp.broadcast_to(packed[:, None, :], (8, 16, 128)).reshape(128, 128)
            ones = jnp.where((words & bit) != 0, 1.0, 0.0)
            unp[base + t] = ones.astype(jnp.bfloat16)
            return 0

        lax.fori_loop(0, tile_count, body, 0, unroll=4)

    def load_features(r, _):
        for h in range(halves):
            block = feat_ref[rep, h, :, pl.ds(pl.multiple_of(r * 128, 128), 128)]
            xs[h, r] = split_rows(block, True)
        return 0

    lax.fori_loop(0, nblocks, load_features, 0, unroll=2)
    unpack_from(tiles_ref, 0)
    tile_copy.wait()
    unpack_from(tiles_in, tile_count)

    def sweep(order, source_of, keep, source, h, transposed, first, span=None):
        rows = 2 * ch + (16 if first else 0)
        dims = (((1,), (1 if transposed else 0,)), ((), ()))

        def step(g, running):
            base = g * UNROLL
            fresh = []
            for u in range(UNROLL):
                product = lax.dot_general(
                    source[h, source_of[base + u]][:rows], unp[order[base + u]], dims,
                    preferred_element_type=jnp.float32,
                )
                value = product[:ch] + product[ch:2 * ch]
                if first:
                    value = jnp.concatenate([value, product[2 * ch:2 * ch + 8]], axis=0)
                fresh.append(value)
            for u in range(UNROLL):
                running = running * keep[base + u] + fresh[u]
                fresh[u] = running
            for u in range(UNROLL):
                run_sums[base + u, :ch + (8 if first else 0)] = fresh[u]
            return running

        start = jnp.zeros((ch + (8 if first else 0), 128), jnp.float32)
        groups = total_tiles // UNROLL
        if span is None:
            lax.fori_loop(0, groups, step, start)
            return
        phase, low, high = span
        count = high - low

        def outer(s, running):
            exchange_step(phase, low + s)
            return lax.fori_loop(s * groups // count, (s + 1) * groups // count, step, running)

        lax.fori_loop(0, count, outer, start)

    def remote(source, target, send, recv, where):
        return pltpu.make_async_remote_copy(
            src_ref=source, dst_ref=target, send_sem=send, recv_sem=recv,
            device_id={"node": where}, device_id_type=MESH,
        )

    def copy_right(turn, k):
        part = pl.ds(k * per, per)
        return remote(to_right.at[turn, part], in_left.at[turn, part],
                      send_r.at[turn, k], recv_l.at[turn, k], right)

    def copy_left(turn, k):
        part = pl.ds(k * per, per)
        return remote(to_left.at[turn, part], in_right.at[turn, part],
                      send_l.at[turn, k], recv_r.at[turn, k], left)

    deg_right_copy = remote(deg_to_right, deg_left, deg_sem.at[0], deg_sem.at[1], right)
    deg_left_copy = remote(deg_to_left, deg_right, deg_sem.at[2], deg_sem.at[3], left)

    def pass_on(turn, h, k, first, sends, receives, copy_of, to_there, from_there, deg_copy,
                deg_to_there, deg_from_there):
        part = pl.ds(k * per, per)

        def degrees_too(act):
            if first:
                pl.when(k == 0)(act)

        @pl.when(receives)
        def _():
            degrees_too(lambda: deg_copy.wait_recv())
            copy_of(turn, k).wait_recv()

        @pl.when(sends)
        def _():
            def send_degrees():
                deg_to_there[...] = own_deg[...] + deg_from_there[...]
                deg_copy.start()

            degrees_too(send_degrees)
            to_there[turn, part] = own[h, part] + from_there[turn, part]
            copy_of(turn, k).start()

    def go_right(phase, k):
        pass_on(phase, phase % halves, k, phase == 0, has_right, has_left, copy_right, to_right,
                in_left, deg_right_copy, deg_to_right, deg_left)

    def go_left(phase, k):
        pass_on(phase, phase % halves, k, phase == 0, has_left, has_right, copy_left, to_left,
                in_right, deg_left_copy, deg_to_left, deg_right)

    def every_chunk(move, phase):
        def one(k, _):
            move(phase, k)
            return 0

        lax.fori_loop(0, CHUNKS, one, 0)

    def exchange_start(phase):
        pl.when(jnp.logical_not(has_left))(lambda: every_chunk(go_right, phase))
        pl.when(jnp.logical_not(has_right))(lambda: every_chunk(go_left, phase))

    def exchange_step(phase, s):
        k_right = s - HOP * (pos - 1)
        k_left = s - HOP * (n_node - 2 - pos)
        inner = has_left & has_right

        @pl.when(inner & (k_right >= 0) & (k_right < CHUNKS))
        def _():
            go_right(phase, k_right)

        @pl.when(inner & (k_left >= 0) & (k_left < CHUNKS))
        def _():
            go_left(phase, k_left)

    def exchange_end(phase):
        pl.when(jnp.logical_not(has_right))(lambda: every_chunk(go_right, phase))
        pl.when(jnp.logical_not(has_left))(lambda: every_chunk(go_left, phase))

    steps = CHUNKS + HOP * max(n_node - 2, 0)

    def push(turn, h, span=None):
        first = turn == 0 and h == 0
        sweep(order_e, row_e, keep_e, xs, h, False, first, span)

        def take_edges(b, _):
            found = run_sums[last_e[b]]
            own[h, b] = found[:ch]
            if first:
                own_deg[pl.ds(b, 1)] = found[ch:ch + 1]
            return 0

        lax.fori_loop(0, edge_blocks, take_edges, 0, unroll=4)
        exchange_start(turn * halves + h)

    def pull(turn, h, span=None):
        first = turn == 0 and h == 0
        phase = turn * halves + h
        exchange_end(phase)
        if first:
            degree = own_deg[...] + deg_left[...] + deg_right[...]
            edge_inv[...] = 1.0 / jnp.maximum(degree, 1.0)

        def means(b, _):
            edge_sum = own[h, b] + in_left[phase, b] + in_right[phase, b]
            ms[h, b] = split_rows(edge_sum * edge_inv[pl.ds(b, 1)], True)
            return 0

        lax.fori_loop(0, edge_blocks, means, 0, unroll=4)
        sweep(order_r, edge_r, keep_r, ms, h, True, first, span)

        def new_block(r):
            found = run_sums[last_r[r]]
            if first:
                node_floor[r] = jnp.maximum(found[ch:ch + 8], 1.0)
            lanes = pl.ds(pl.multiple_of(r * 128, 128), 128)
            block = feat_ref[rep, h, :, lanes]
            return lanes, (1.0 - teleport) * (found[:ch] / node_floor[r][:1]) + teleport * block

        if turn < ROUNDS - 1:
            def next_x(r, _):
                xs[h, r] = split_rows(new_block(r)[1], True)
                return 0

            lax.fori_loop(0, nblocks, next_x, 0, unroll=4)
            return []
        group = nblocks // OUT_CHUNKS
        copies = []
        for k in range(OUT_CHUNKS):
            def last_x(r, _):
                lanes, value = new_block(r)
                out_ref[rep, h, :, lanes] = value
                return 0

            lax.fori_loop(k * group, (k + 1) * group, last_x, 0, unroll=4)
            lanes = pl.ds(k * group * 128, group * 128)
            copy = pltpu.make_async_remote_copy(
                src_ref=out_ref.at[rep, h, :, lanes], dst_ref=out_ref.at[rep, h, :, lanes],
                send_sem=out_send.at[h, k], recv_sem=out_recv.at[h, k],
                device_id={"rep": 1 - rep}, device_id_type=MESH,
            )
            copy.start()
            copies.append(copy)
        return copies

    @pl.when(jnp.logical_not(has_left))
    def _():
        in_left[...] = jnp.zeros_like(in_left)
        deg_left[...] = jnp.zeros_like(deg_left)

    @pl.when(jnp.logical_not(has_right))
    def _():
        in_right[...] = jnp.zeros_like(in_right)
        deg_right[...] = jnp.zeros_like(deg_right)

    for h in range(halves):
        ms[h, edge_blocks] = jnp.concatenate(
            [jnp.zeros((2 * ch, 128), jnp.float32), jnp.ones((16, 128), jnp.float32)], axis=0
        ).astype(jnp.bfloat16)

    copies = []
    if halves == 1:
        for turn in range(ROUNDS):
            push(turn, 0)

            def alone(s, _, turn=turn):
                exchange_step(turn, s)
                return 0

            lax.fori_loop(0, steps, alone, 0)
            copies += pull(turn, 0)
    else:
        cut = steps // 2
        push(0, 0)
        push(0, 1, (0, 0, steps))
        for turn in range(ROUNDS):
            for h in range(2):
                phase = 2 * turn + h + 1
                if turn < ROUNDS - 1:
                    copies += pull(turn, h, (phase, 0, cut))
                    push(turn + 1, h, (phase, cut, steps))
                else:
                    copies += pull(turn, h, (phase, 0, steps) if h == 0 else None)

    for phase in range(ROUNDS * halves):
        def sent(k, _, phase=phase):
            @pl.when(has_right)
            def _():
                copy_right(phase, k).wait_send()

            @pl.when(has_left)
            def _():
                copy_left(phase, k).wait_send()

            return 0

        lax.fori_loop(0, CHUNKS, sent, 0)

    @pl.when(has_right)
    def _():
        deg_right_copy.wait_send()

    @pl.when(has_left)
    def _():
        deg_left_copy.wait_send()

    for copy in copies:
        copy.wait()


def shards(features, tile_rows, tile_slot, slot_block, tiles):
    n_node = lax.axis_size("node")
    channels, row_count = features.shape
    nblocks = row_count // 128
    tile_count = tile_rows.shape[0]
    total = 2 * tile_count
    halves = 2 if channels % 32 == 0 else 1
    ch = channels // 2 // halves
    phases = ROUNDS * halves
    edge_blocks = n_node * EB_DEV

    slots = slot_block.reshape(-1)
    slot_of = jnp.arange(slots.shape[0], dtype=jnp.int32)
    slot_edge = jnp.where(slots >= 0, slot_of // CAP * EB_DEV + slots, edge_blocks)
    edges = jnp.sum(jnp.where(tile_slot[:, None] == slot_of[None, :], slot_edge[None, :], 0), axis=1)
    mine = jnp.concatenate([tile_rows, edges.astype(jnp.int32)])
    theirs = lax.ppermute(mine, "rep", [(0, 1), (1, 0)])
    rows = jnp.concatenate([mine[:tile_count], theirs[:tile_count]])
    edges = jnp.concatenate([mine[tile_count:], theirs[tile_count:]])
    ids = jnp.arange(total, dtype=jnp.int32)

    def arrange(key, other, groups):
        full = key * total + ids
        rank = jnp.sum((full[None, :] < full[:, None]).astype(jnp.int32), axis=1)
        hot = rank[None, :] == ids[:, None]
        order = jnp.sum(jnp.where(hot, ids[None, :], 0), axis=1)
        source = jnp.sum(jnp.where(hot, other[None, :], 0), axis=1)
        first = jnp.sum((key[None, :] == key[:, None]) & (full[None, :] < full[:, None]), axis=1) == 0
        keep = jnp.sum(jnp.where(hot & ~first[None, :], 1.0, 0.0), axis=1)
        group = jnp.arange(groups, dtype=jnp.int32)
        upto = jnp.sum((key[None, :] <= group[:, None]).astype(jnp.int32), axis=1)
        some = jnp.any(key[None, :] == group[:, None], axis=1)
        return order, source, keep, jnp.where(some, upto - 1, total)

    order_e, row_e, keep_e, last_e = arrange(edges, rows, edge_blocks)
    order_r, edge_r, keep_r, last_r = arrange(rows, edges, nblocks)

    smem = pl.BlockSpec(memory_space=pltpu.SMEM)
    vmem = pl.BlockSpec(memory_space=pltpu.VMEM)
    f32, bf16 = jnp.float32, jnp.bfloat16
    wide = (edge_blocks, ch, 128)
    deg = (edge_blocks, 128)
    dma = pltpu.SemaphoreType.DMA
    out = pl.pallas_call(
        functools.partial(kernel, n_node),
        out_shape=jax.ShapeDtypeStruct((2, halves, ch, row_count), f32),
        in_specs=[smem] * 8 + [vmem] * 2,
        out_specs=vmem,
        scratch_shapes=[
            pltpu.VMEM((tile_count, 8, 128), jnp.int32),
            pltpu.VMEM((total, 128, 128), bf16),
            pltpu.VMEM((halves, nblocks, 2 * ch + 16, 128), bf16),
            pltpu.VMEM((halves, edge_blocks + 1, 2 * ch + 16, 128), bf16),
            pltpu.VMEM((total + 1, ch + 8, 128), f32),
            pltpu.VMEM((halves,) + wide, f32),
            pltpu.VMEM((phases,) + wide, f32),
            pltpu.VMEM((phases,) + wide, f32),
            pltpu.VMEM((phases,) + wide, f32),
            pltpu.VMEM((phases,) + wide, f32),
            pltpu.VMEM(deg, f32),
            pltpu.VMEM(deg, f32),
            pltpu.VMEM(deg, f32),
            pltpu.VMEM(deg, f32),
            pltpu.VMEM(deg, f32),
            pltpu.VMEM((nblocks, 8, 128), f32),
            pltpu.VMEM(deg, f32),
            dma((2,)),
            dma((halves, OUT_CHUNKS)),
            dma((halves, OUT_CHUNKS)),
            dma((phases, CHUNKS)),
            dma((phases, CHUNKS)),
            dma((phases, CHUNKS)),
            dma((phases, CHUNKS)),
            dma((4,)),
        ],
        compiler_params=pltpu.CompilerParams(
            collective_id=0, has_side_effects=True, vmem_limit_bytes=48 * 1024 * 1024
        ),
    )(order_e, row_e, keep_e, last_e, order_r, edge_r, keep_r, last_r,
      features.reshape(2, halves, ch, row_count), tiles)
    return out.reshape(channels, row_count)


def solution(mesh):
    return jax.shard_map(
        shards,
        mesh=mesh,
        in_specs=(
            P("chan", ("parts", "node")),
            P(("parts", "node", "rep")),
            P(("parts", "node", "rep")),
            P(("parts", "node", "rep"), None),
            P(("parts", "node", "rep"), None, None),
        ),
        out_specs=P("chan", ("parts", "node")),
        check_vma=False,
    )
```

```python
import functools

import jax
import jax.numpy as jnp
from jax import lax
from jax.experimental import pallas as pl
from jax.experimental.pallas import tpu as pltpu
from jax.sharding import PartitionSpec as P

EB_DEV = 12
CAP = 6
ROUNDS = 2
CHUNKS = 8
HOP = 6
OUT_CHUNKS = 2
UNROLL = 32
MESH = pl.DeviceIdType.MESH
teleport = 0.1


def split_rows(value, ones):
    high = value.astype(jnp.bfloat16).astype(jnp.float32)
    parts = [high, value - high]
    if ones:
        parts.append(jnp.ones((16, 128), jnp.float32))
    return jnp.concatenate(parts, axis=0).astype(jnp.bfloat16)


def kernel(
    n_node,
    order_e, row_e, keep_e, last_e, order_r, edge_r, keep_r, last_r,
    feat_ref, tiles_ref,
    out_ref,
    tiles_in, unp, xs, ms, run_sums, own, in_left, in_right, to_left, to_right,
    own_deg, deg_left, deg_right, deg_to_left, deg_to_right, node_floor, edge_inv,
    tile_sem, out_send, out_recv, send_l, send_r, recv_l, recv_r, deg_sem,
):
    halves, ch = feat_ref.shape[1:3]
    tile_count = tiles_ref.shape[0]
    total_tiles = 2 * tile_count
    nblocks = feat_ref.shape[3] // 128
    edge_blocks = own.shape[1]
    per = edge_blocks // CHUNKS
    pos = lax.axis_index("node")
    rep = lax.axis_index("rep")
    left, right = pos - 1, pos + 1
    has_left = pos > 0
    has_right = pos < n_node - 1

    barrier = pltpu.get_barrier_semaphore()
    pl.semaphore_signal(barrier, inc=1, device_id={"rep": 1 - rep}, device_id_type=MESH)

    @pl.when(has_left)
    def _():
        pl.semaphore_signal(barrier, inc=1, device_id={"node": left}, device_id_type=MESH)

    @pl.when(has_right)
    def _():
        pl.semaphore_signal(barrier, inc=1, device_id={"node": right}, device_id_type=MESH)

    pl.semaphore_wait(barrier, 1 + jnp.where(has_left, 1, 0) + jnp.where(has_right, 1, 0))

    tile_copy = pltpu.make_async_remote_copy(
        src_ref=tiles_ref, dst_ref=tiles_in, send_sem=tile_sem.at[0], recv_sem=tile_sem.at[1],
        device_id={"rep": 1 - rep}, device_id_type=MESH,
    )
    tile_copy.start()

    zero_rows = jnp.zeros(run_sums.shape[1:], jnp.float32)
    run_sums[total_tiles] = zero_rows
    bit = jnp.left_shift(1, lax.broadcasted_iota(jnp.int32, (128, 128), 0) & 15)

    def unpack_from(source, base):
        def body(t, _):
            packed = source[t]
            words = jnp.broadcast_to(packed[:, None, :], (8, 16, 128)).reshape(128, 128)
            ones = jnp.where((words & bit) != 0, 1.0, 0.0)
            unp[base + t] = ones.astype(jnp.bfloat16)
            return 0

        lax.fori_loop(0, tile_count, body, 0, unroll=4)

    def load_features(r, _):
        for h in range(halves):
            block = feat_ref[rep, h, :, pl.ds(pl.multiple_of(r * 128, 128), 128)]
            xs[h, r] = split_rows(block, True)
        return 0

    lax.fori_loop(0, nblocks, load_features, 0, unroll=2)
    unpack_from(tiles_ref, 0)
    tile_copy.wait()
    unpack_from(tiles_in, tile_count)

    def sweep(order, source_of, keep, source, h, transposed, first, span=None):
        rows = 2 * ch + (16 if first else 0)
        dims = (((1,), (1 if transposed else 0,)), ((), ()))

        def step(g, running):
            base = g * UNROLL
            fresh = []
            for u in range(UNROLL):
                product = lax.dot_general(
                    source[h, source_of[base + u]][:rows], unp[order[base + u]], dims,
                    preferred_element_type=jnp.float32,
                )
                value = product[:ch] + product[ch:2 * ch]
                if first:
                    value = jnp.concatenate([value, product[2 * ch:2 * ch + 8]], axis=0)
                fresh.append(value)
            for u in range(UNROLL):
                running = running * keep[base + u] + fresh[u]
                fresh[u] = running
            for u in range(UNROLL):
                run_sums[base + u, :ch + (8 if first else 0)] = fresh[u]
            return running

        start = jnp.zeros((ch + (8 if first else 0), 128), jnp.float32)
        groups = total_tiles // UNROLL
        if span is None:
            lax.fori_loop(0, groups, step, start)
            return
        phase, low, high = span
        count = high - low

        def outer(s, running):
            exchange_step(phase, low + s)
            return lax.fori_loop(s * groups // count, (s + 1) * groups // count, step, running)

        lax.fori_loop(0, count, outer, start)

    def remote(source, target, send, recv, where):
        return pltpu.make_async_remote_copy(
            src_ref=source, dst_ref=target, send_sem=send, recv_sem=recv,
            device_id={"node": where}, device_id_type=MESH,
        )

    def copy_right(turn, k):
        part = pl.ds(k * per, per)
        return remote(to_right.at[turn, part], in_left.at[turn, part],
                      send_r.at[turn, k], recv_l.at[turn, k], right)

    def copy_left(turn, k):
        part = pl.ds(k * per, per)
        return remote(to_left.at[turn, part], in_right.at[turn, part],
                      send_l.at[turn, k], recv_r.at[turn, k], left)

    deg_right_copy = remote(deg_to_right, deg_left, deg_sem.at[0], deg_sem.at[1], right)
    deg_left_copy = remote(deg_to_left, deg_right, deg_sem.at[2], deg_sem.at[3], left)

    def pass_on(turn, h, k, first, sends, receives, copy_of, to_there, from_there, deg_copy,
                deg_to_there, deg_from_there):
        part = pl.ds(k * per, per)

        def degrees_too(act):
            if first:
                pl.when(k == 0)(act)

        @pl.when(receives)
        def _():
            degrees_too(lambda: deg_copy.wait_recv())
            copy_of(turn, k).wait_recv()

        @pl.when(sends)
        def _():
            def send_degrees():
                deg_to_there[...] = own_deg[...] + deg_from_there[...]
                deg_copy.start()

            degrees_too(send_degrees)
            to_there[turn, part] = own[h, part] + from_there[turn, part]
            copy_of(turn, k).start()

    def go_right(phase, k):
        pass_on(phase, phase % halves, k, phase == 0, has_right, has_left, copy_right, to_right,
                in_left, deg_right_copy, deg_to_right, deg_left)

    def go_left(phase, k):
        pass_on(phase, phase % halves, k, phase == 0, has_left, has_right, copy_left, to_left,
                in_right, deg_left_copy, deg_to_left, deg_right)

    def every_chunk(move, phase):
        def one(k, _):
            move(phase, k)
            return 0

        lax.fori_loop(0, CHUNKS, one, 0)

    def exchange_start(phase):
        pl.when(jnp.logical_not(has_left))(lambda: every_chunk(go_right, phase))
        pl.when(jnp.logical_not(has_right))(lambda: every_chunk(go_left, phase))

    def exchange_step(phase, s):
        k_right = s - HOP * (pos - 1)
        k_left = s - HOP * (n_node - 2 - pos)
        inner = has_left & has_right

        @pl.when(inner & (k_right >= 0) & (k_right < CHUNKS))
        def _():
            go_right(phase, k_right)

        @pl.when(inner & (k_left >= 0) & (k_left < CHUNKS))
        def _():
            go_left(phase, k_left)

    def exchange_end(phase):
        pl.when(jnp.logical_not(has_right))(lambda: every_chunk(go_right, phase))
        pl.when(jnp.logical_not(has_left))(lambda: every_chunk(go_left, phase))

    steps = CHUNKS + HOP * max(n_node - 2, 0)

    def push(turn, h, span=None):
        first = turn == 0 and h == 0
        sweep(order_e, row_e, keep_e, xs, h, False, first, span)

        def take_edges(b, _):
            found = run_sums[last_e[b]]
            own[h, b] = found[:ch]
            if first:
                own_deg[pl.ds(b, 1)] = found[ch:ch + 1]
            return 0

        lax.fori_loop(0, edge_blocks, take_edges, 0, unroll=4)
        exchange_start(turn * halves + h)

    def pull(turn, h, span=None):
        first = turn == 0 and h == 0
        phase = turn * halves + h
        exchange_end(phase)
        if first:
            degree = own_deg[...] + deg_left[...] + deg_right[...]
            edge_inv[...] = 1.0 / jnp.maximum(degree, 1.0)

        def means(b, _):
            edge_sum = own[h, b] + in_left[phase, b] + in_right[phase, b]
            ms[h, b] = split_rows(edge_sum * edge_inv[pl.ds(b, 1)], True)
            return 0

        lax.fori_loop(0, edge_blocks, means, 0, unroll=4)
        sweep(order_r, edge_r, keep_r, ms, h, True, first, span)

        def new_block(r):
            found = run_sums[last_r[r]]
            if first:
                node_floor[r] = jnp.maximum(found[ch:ch + 8], 1.0)
            lanes = pl.ds(pl.multiple_of(r * 128, 128), 128)
            block = feat_ref[rep, h, :, lanes]
            return lanes, (1.0 - teleport) * (found[:ch] / node_floor[r][:1]) + teleport * block

        if turn < ROUNDS - 1:
            def next_x(r, _):
                xs[h, r] = split_rows(new_block(r)[1], True)
                return 0

            lax.fori_loop(0, nblocks, next_x, 0, unroll=4)
            return []
        group = nblocks // OUT_CHUNKS
        copies = []
        for k in range(OUT_CHUNKS):
            def last_x(r, _):
                lanes, value = new_block(r)
                out_ref[rep, h, :, lanes] = value
                return 0

            lax.fori_loop(k * group, (k + 1) * group, last_x, 0, unroll=4)
            lanes = pl.ds(k * group * 128, group * 128)
            copy = pltpu.make_async_remote_copy(
                src_ref=out_ref.at[rep, h, :, lanes], dst_ref=out_ref.at[rep, h, :, lanes],
                send_sem=out_send.at[h, k], recv_sem=out_recv.at[h, k],
                device_id={"rep": 1 - rep}, device_id_type=MESH,
            )
            copy.start()
            copies.append(copy)
        return copies

    @pl.when(jnp.logical_not(has_left))
    def _():
        in_left[...] = jnp.zeros_like(in_left)
        deg_left[...] = jnp.zeros_like(deg_left)

    @pl.when(jnp.logical_not(has_right))
    def _():
        in_right[...] = jnp.zeros_like(in_right)
        deg_right[...] = jnp.zeros_like(deg_right)

    for h in range(halves):
        ms[h, edge_blocks] = jnp.concatenate(
            [jnp.zeros((2 * ch, 128), jnp.float32), jnp.ones((16, 128), jnp.float32)], axis=0
        ).astype(jnp.bfloat16)

    copies = []
    if halves == 1:
        for turn in range(ROUNDS):
            push(turn, 0)

            def alone(s, _, turn=turn):
                exchange_step(turn, s)
                return 0

            lax.fori_loop(0, steps, alone, 0)
            copies += pull(turn, 0)
    else:
        cut = steps // 2
        push(0, 0)
        push(0, 1, (0, 0, steps))
        for turn in range(ROUNDS):
            for h in range(2):
                phase = 2 * turn + h + 1
                if turn < ROUNDS - 1:
                    copies += pull(turn, h, (phase, 0, cut))
                    push(turn + 1, h, (phase, cut, steps))
                else:
                    copies += pull(turn, h, (phase, 0, steps) if h == 0 else None)

    for phase in range(ROUNDS * halves):
        def sent(k, _, phase=phase):
            @pl.when(has_right)
            def _():
                copy_right(phase, k).wait_send()

            @pl.when(has_left)
            def _():
                copy_left(phase, k).wait_send()

            return 0

        lax.fori_loop(0, CHUNKS, sent, 0)

    @pl.when(has_right)
    def _():
        deg_right_copy.wait_send()

    @pl.when(has_left)
    def _():
        deg_left_copy.wait_send()

    for copy in copies:
        copy.wait()


def shards(features, tile_rows, tile_slot, slot_block, tiles):
    n_node = lax.axis_size("node")
    channels, row_count = features.shape
    nblocks = row_count // 128
    tile_count = tile_rows.shape[0]
    total = 2 * tile_count
    halves = 2 if channels % 32 == 0 else 1
    ch = channels // 2 // halves
    phases = ROUNDS * halves
    edge_blocks = n_node * EB_DEV

    slots = slot_block.reshape(-1)
    slot_of = jnp.arange(slots.shape[0], dtype=jnp.int32)
    slot_edge = jnp.where(slots >= 0, slot_of // CAP * EB_DEV + slots, edge_blocks)
    edges = jnp.sum(jnp.where(tile_slot[:, None] == slot_of[None, :], slot_edge[None, :], 0), axis=1)
    mine = jnp.concatenate([tile_rows, edges.astype(jnp.int32)])
    theirs = lax.ppermute(mine, "rep", [(0, 1), (1, 0)])
    rows = jnp.concatenate([mine[:tile_count], theirs[:tile_count]])
    edges = jnp.concatenate([mine[tile_count:], theirs[tile_count:]])
    ids = jnp.arange(total, dtype=jnp.int32)

    def arrange(key, other, groups):
        full = key * total + ids
        rank = jnp.sum((full[None, :] < full[:, None]).astype(jnp.int32), axis=1)
        hot = rank[None, :] == ids[:, None]
        order = jnp.sum(jnp.where(hot, ids[None, :], 0), axis=1)
        source = jnp.sum(jnp.where(hot, other[None, :], 0), axis=1)
        first = jnp.sum((key[None, :] == key[:, None]) & (full[None, :] < full[:, None]), axis=1) == 0
        keep = jnp.sum(jnp.where(hot & ~first[None, :], 1.0, 0.0), axis=1)
        group = jnp.arange(groups, dtype=jnp.int32)
        upto = jnp.sum((key[None, :] <= group[:, None]).astype(jnp.int32), axis=1)
        some = jnp.any(key[None, :] == group[:, None], axis=1)
        return order, source, keep, jnp.where(some, upto - 1, total)

    order_e, row_e, keep_e, last_e = arrange(edges, rows, edge_blocks)
    order_r, edge_r, keep_r, last_r = arrange(rows, edges, nblocks)

    smem = pl.BlockSpec(memory_space=pltpu.SMEM)
    vmem = pl.BlockSpec(memory_space=pltpu.VMEM)
    f32, bf16 = jnp.float32, jnp.bfloat16
    wide = (edge_blocks, ch, 128)
    deg = (edge_blocks, 128)
    dma = pltpu.SemaphoreType.DMA
    out = pl.pallas_call(
        functools.partial(kernel, n_node),
        out_shape=jax.ShapeDtypeStruct((2, halves, ch, row_count), f32),
        in_specs=[smem] * 8 + [vmem] * 2,
        out_specs=vmem,
        scratch_shapes=[
            pltpu.VMEM((tile_count, 8, 128), jnp.int32),
            pltpu.VMEM((total, 128, 128), bf16),
            pltpu.VMEM((halves, nblocks, 2 * ch + 16, 128), bf16),
            pltpu.VMEM((halves, edge_blocks + 1, 2 * ch + 16, 128), bf16),
            pltpu.VMEM((total + 1, ch + 8, 128), f32),
            pltpu.VMEM((halves,) + wide, f32),
            pltpu.VMEM((phases,) + wide, f32),
            pltpu.VMEM((phases,) + wide, f32),
            pltpu.VMEM((phases,) + wide, f32),
            pltpu.VMEM((phases,) + wide, f32),
            pltpu.VMEM(deg, f32),
            pltpu.VMEM(deg, f32),
            pltpu.VMEM(deg, f32),
            pltpu.VMEM(deg, f32),
            pltpu.VMEM(deg, f32),
            pltpu.VMEM((nblocks, 8, 128), f32),
            pltpu.VMEM(deg, f32),
            dma((2,)),
            dma((halves, OUT_CHUNKS)),
            dma((halves, OUT_CHUNKS)),
            dma((phases, CHUNKS)),
            dma((phases, CHUNKS)),
            dma((phases, CHUNKS)),
            dma((phases, CHUNKS)),
            dma((4,)),
        ],
        compiler_params=pltpu.CompilerParams(
            collective_id=0, has_side_effects=True, vmem_limit_bytes=48 * 1024 * 1024
        ),
    )(order_e, row_e, keep_e, last_e, order_r, edge_r, keep_r, last_r,
      features.reshape(2, halves, ch, row_count), tiles)
    return out.reshape(channels, row_count)


def solution(mesh):
    return jax.shard_map(
        shards,
        mesh=mesh,
        in_specs=(
            P("chan", ("parts", "node")),
            P(("parts", "node", "rep")),
            P(("parts", "node", "rep")),
            P(("parts", "node", "rep"), None),
            P(("parts", "node", "rep"), None, None),
        ),
        out_specs=P("chan", ("parts", "node")),
        check_vma=False,
    )
```
